512 devices in a mesh: row: 16 (over y, core), col: 32 (over z, x).
Axes of the slice: x: 4, y: 8, z: 8, core: 2. Of those that a mesh axis runs over, the one named last changes fastest.
Arguments:
- points: float32 [96, 40960], P(None, ('row', 'col')), may hold values from -3 to 3
- scales: float32 [96], replicated, may hold values from 0.0001 to 1
- solution: float32 [97, 40960], P(None, ('row', 'col')), may hold values from -250 to 250
- residual: float32 [97, 40960], P(None, ('row', 'col')), may hold values from -250 to 250
- direction: float32 [97, 40960], P(None, ('row', 'col')), may hold values from -250 to 250
Outputs:
- solution_next: float32 [97, 40960], P(None, ('row', 'col'))
- residual_next: float32 [97, 40960], P(None, ('row', 'col'))
- direction_next: float32 [97, 40960], P(None, ('row', 'col'))
The draws below stay inside these ranges and needn't reach their ends.
All inputs are finite; a program needn't handle non-finite values.
Results may differ from the reference program's by a relative error of at most 0.00018.
Values sent between devices are 32-bit elements; how exact they have to be, the bound alone decides.
A program may use at most 64 MiB of HBM per device.

```python
import math
import jax
import jax.numpy as jnp
from jax import lax

D = 96
SAMPLES = 40960


def state_field(key, base_draw, ramp_top):
    key_comp, key_sample = jax.random.split(key, 2)
    comp_scale = jnp.exp(jax.random.uniform(key_comp, (D + 1, 1), jnp.float32, jnp.log(0.3), jnp.log(3.0)))
    sample_scale = jnp.exp(jax.random.uniform(key_sample, (1, SAMPLES), jnp.float32, jnp.log(0.3), jnp.log(3.0)))
    ramp_line = 1.0 + (ramp_top - 1.0) * jnp.arange(SAMPLES, dtype=jnp.float32)[None, :] / max(SAMPLES - 1, 1)
    return (base_draw * comp_scale * sample_scale * ramp_line).astype(jnp.float32)


def draw_solution(key, part):
    key = jax.random.fold_in(key, 11)
    key_base, key_rest = jax.random.split(key)
    base_draw = jax.random.truncated_normal(key_base, -4.0, 4.0, (D + 1, SAMPLES), jnp.float32)
    return state_field(key_rest, base_draw, 3.0)


def draw_residual(key, part):
    key = jax.random.fold_in(key, 23)
    key_base, key_rest = jax.random.split(key)
    base_draw = jax.random.truncated_normal(key_base, -4.0, 4.0, (D + 1, SAMPLES), jnp.float32)
    return state_field(key_rest, base_draw, 3.0)


def draw_direction(key, part):
    key = jax.random.fold_in(key, 37)
    key_base, key_rest = jax.random.split(key)
    base_draw = jax.random.truncated_normal(key_base, -4.0, 4.0, (D + 1, SAMPLES), jnp.float32)
    return state_field(key_rest, base_draw, 3.0)


def block_scale(key, shape, pieces, smallest, top_value):
    gain, own = 1.0, jax.random.fold_in(key, 6)
    for position, shards_of in pieces:
        draws = jnp.exp(jax.random.uniform(jax.random.fold_in(own, position), (shards_of,), jnp.float32, smallest / len(pieces), top_value / len(pieces)))
        gain = gain * jnp.repeat(draws, shape[position] // shards_of).reshape([-1 if axis == position else 1 for axis in range(len(shape))])
    return gain


def centred(stream_key, extent, width, reach, pieces=(), kind=jnp.bfloat16):
    values = jax.random.normal(stream_key, extent, jnp.float32) * width
    if len(pieces) > 0:
        values = block_scale(stream_key, extent, pieces, -0.22, 0.18) * values
    return jnp.clip(values, min=-reach, max=reach).astype(kind)


def setup_inputs(seed: int = 0) -> dict:
    arg_keys = jax.random.split(jax.random.key(seed), 6)
    return {
        "points": centred(arg_keys[0], (D, SAMPLES), 0.5, 3.0, ((1, 512),), jnp.float32),
        "scales": jnp.clip(jnp.exp(jax.random.uniform(arg_keys[1], (D,), jnp.float32, math.log(0.0001), math.log(1.0))), 0.0001, 1.0),
        "solution": draw_solution(jax.random.fold_in(arg_keys[5], 71), 0),
        "residual": draw_residual(jax.random.fold_in(arg_keys[5], 71), 0),
        "direction": draw_direction(jax.random.fold_in(arg_keys[5], 71), 0),
    }


def contract(left, right, dims):
    return lax.dot_general(left, right, (dims, ((), ())), precision=lax.Precision.HIGHEST, preferred_element_type=jnp.float32)

def kernel_block(row_coords, col_coords, col_values, col_grads, col_square, col_proj):
    products = contract(row_coords, col_coords, ((0,), (0,)))
    row_square = lax.optimization_barrier(jnp.sum(row_coords * row_coords, axis=0))
    kernel = jnp.exp(-0.5 * (row_square[:, None] + col_square[None, :] - 2.0 * products))
    slopes = contract(row_coords, col_grads, ((0,), (0,))) - col_proj[None, :]
    weighted = kernel * (col_values[None, :] + slopes)
    value_out = lax.optimization_barrier(jnp.sum(weighted, axis=1))
    grad_out = -row_coords * value_out[None, :] + contract(col_coords, weighted, ((1,), (1,))) + contract(col_grads, kernel, ((1,), (1,)))
    return jnp.concatenate([value_out[None, :], grad_out], axis=0)

def apply_operator(scaled, field):
    design = scaled.shape[0]
    total = scaled.shape[1]
    col_values = field[0]
    col_grads = field[1:]
    col_square = lax.optimization_barrier(jnp.sum(scaled * scaled, axis=0))
    col_proj = lax.optimization_barrier(jnp.sum(scaled * col_grads, axis=0))
    block_rows = 1024 if total % 1024 == 0 else total
    block_count = total // block_rows
    stacked = jnp.moveaxis(scaled.reshape(design, block_count, block_rows), 1, 0)

    def tile_rows(row_coords):
        return kernel_block(row_coords, scaled, col_values, col_grads, col_square, col_proj)
    result = lax.map(tile_rows, stacked)
    return jnp.moveaxis(result, 0, 1).reshape(design + 1, total)

def reference(points, scales, solution, residual, direction):
    scaled = points * jnp.sqrt(2.0 * scales)[:, None]
    image_field = apply_operator(scaled, direction)
    norm_old = jnp.sum(residual * residual)
    curvature = jnp.sum(direction * image_field)
    step_size = norm_old / curvature
    solution_next = solution + step_size * direction
    residual_next = residual - step_size * image_field
    norm_new = jnp.sum(residual_next * residual_next)
    direction_next = residual_next + norm_new / norm_old * direction
    return (solution_next, residual_next, direction_next)
```

```python
import functools
import math

import jax
import jax.numpy as jnp
from jax import lax
from jax.experimental import pallas as pl
from jax.experimental.pallas import tpu as pltpu
from jax.sharding import PartitionSpec as P

F32, BF16 = jnp.float32, jnp.bfloat16
MESH = pl.DeviceIdType.MESH
DESIGN = 96
LANES = 128
ROOT = math.sqrt(math.log2(math.e))
NT = (((1,), (1,)), ((), ()))
NN = (((1,), (0,)), ((), ()))
NORM, REST, ONE, ONE2 = 97, 98, 99, 100


def dot(a, b, dims):
    return lax.dot_general(a, b, dims, preferred_element_type=F32)


def split(x):
    high = x.astype(BF16)
    return high, (x - high.astype(F32)).astype(BF16)


def joined(x):
    high, low = split(x)
    return high.astype(F32) + low.astype(F32)


def rotate(index, shift, size):
    return lax.rem(index + shift, size)


def kernel(
    dims, block, tile,
    points_ref, scales_ref, solution_ref, residual_ref, direction_ref,
    solution_out, residual_out, direction_out,
    pad_p, pad_d, pad_r, rows, cols, stream,
    prod_hi, prod_lo, slope_hi, slope_lo, mix_w, mix_k,
    partial, from_x, group, from_z, vec, vec_in,
    zs_send, zs_recv, xs_send, xs_recv, ys_send, ys_recv, cs_send, cs_recv,
    xr_send, xr_recv, zr_send, zr_recv, v_send, v_recv,
):
    ny, nc, nz, nx = dims
    per_x = nz * block
    row, col = lax.axis_index("row"), lax.axis_index("col")
    y, core = row // nc, lax.rem(row, nc)
    z, x = col // nx, lax.rem(col, nx)

    def at_z(shift):
        return (row, rotate(z, shift, nz) * nx + x)

    def at_x(shift):
        return (row, z * nx + rotate(x, shift, nx))

    def at_y(shift):
        return (rotate(y, shift, ny) * nc + core, col)

    def at_cx(dc, dx):
        return (y * nc + rotate(core, dc, nc), z * nx + rotate(x, dx, nx))

    peers = [at_z(d) for d in range(1, nz)] + [at_y(d) for d in range(1, ny)]
    peers += [at_cx(c, d) for c in range(nc) for d in range(nx) if c or d]
    barrier = pltpu.get_barrier_semaphore()
    for peer in peers:
        pl.semaphore_signal(barrier, inc=1, device_id=peer, device_id_type=MESH)

    lane = lax.broadcasted_iota(jnp.int32, (LANES, LANES), 1)
    lane_b = lax.broadcasted_iota(jnp.int32, (block, LANES), 1)
    for pad in (pad_p, pad_d, pad_r):
        pad[...] = jnp.zeros_like(pad)
    pad_p[1 : DESIGN + 1, 0:block] = points_ref[...]
    pad_d[0 : DESIGN + 1, 0:block] = direction_ref[...]
    pad_r[0 : DESIGN + 1, 0:block] = residual_ref[...]
    inside = (lane_b >= 1) & (lane_b <= DESIGN)
    coords = pad_p[...].T[0:block] * (jnp.sqrt(2.0 * scales_ref[...]) * ROOT)
    coords = joined(coords)
    norm = -0.5 * jnp.sum(coords * coords, axis=1, keepdims=True)
    norm_main = joined(norm)
    own_row = jnp.where(inside, coords, 0.0)
    own_row = jnp.where(lane_b == NORM, norm_main, own_row)
    own_row = jnp.where(lane_b == REST, norm - norm_main, own_row)
    own_row = jnp.where((lane_b == ONE) | (lane_b == ONE2), 1.0, own_row)
    field = pad_d[...].T[0:block]
    grads = joined(jnp.where(inside, field * (1.0 / ROOT), 0.0))
    value = field[:, 0:1] - jnp.sum(coords * grads, axis=1, keepdims=True)
    value_main = joined(value)
    own_col = jnp.where(lane_b == ONE, value_main, grads)
    own_col = jnp.where(lane_b == ONE2, value - value_main, own_col)
    rows[0:block] = own_row
    cols[0, 0, 0:block] = own_row
    cols[0, 0, block:] = own_col

    pl.semaphore_wait(barrier, len(peers))

    def copy(src, dst, send, recv, peer):
        return pltpu.make_async_remote_copy(
            src_ref=src, dst_ref=dst, send_sem=send, recv_sem=recv, device_id=peer, device_id_type=MESH
        )

    def z_gather(d):
        return copy(
            rows.at[pl.ds(0, block)], rows.at[pl.ds(d * block, block)],
            zs_send.at[d], zs_recv.at[d], at_z(nz - d),
        )

    def y_gather(d):
        return copy(cols.at[0, 0], cols.at[0, d], ys_send.at[d], ys_recv.at[d], at_y(ny - d))

    def x_gather(d):
        return copy(
            rows.at[pl.ds(0, per_x)], rows.at[pl.ds(d * per_x, per_x)],
            xs_send.at[d], xs_recv.at[d], at_x(nx - d),
        )

    def c_gather(d):
        return copy(cols.at[0], cols.at[d], cs_send.at[d], cs_recv.at[d], at_cx(nc - d, 0))

    for d in range(1, nz):
        z_gather(d).start()
    for d in range(1, ny):
        y_gather(d).start()
    for d in range(1, nz):
        z_gather(d).wait_recv()
    for d in range(1, nx):
        x_gather(d).start()
    for d in range(1, ny):
        y_gather(d).wait_recv()
    for d in range(1, nc):
        c_gather(d).start()

    def factors(b, _):
        here = pl.ds(pl.multiple_of(b * block, block), block)
        sample = cols[b // ny, lax.rem(b, ny), 0:block]
        slope = cols[b // ny, lax.rem(b, ny), block:]
        other = jnp.where(lane_b < NORM, sample, pltpu.roll(sample, 2, 1))
        other = jnp.where((lane_b == NORM) | (lane_b == REST), 1.0, other)
        high, low = split(other)
        prod_hi[here, 0:LANES], prod_hi[here, LANES:] = high, high
        prod_lo[here, 0:LANES], prod_lo[here, LANES:] = low, low
        high, low = split(slope)
        slope_hi[here, 0:LANES], slope_hi[here, LANES:] = high, high
        slope_lo[here, 0:LANES], slope_lo[here, LANES:] = low, low
        high, low = split(jnp.where(lane_b == 0, 1.0, sample))
        mix_w[here, 0:LANES], mix_w[here, LANES:] = high, low
        high, low = split(slope * (ROOT * ROOT))
        mix_k[here, 0:LANES], mix_k[here, LANES:] = high, low
        return 0

    lax.fori_loop(0, ny, factors, 0)
    for d in range(1, nc):
        c_gather(d).wait_recv()
    lax.fori_loop(ny, ny * nc, factors, 0)
    for d in range(1, nx):
        x_gather(d).wait_recv()

    def x_reduce(k):
        return copy(partial.at[k], from_x.at[k], xr_send.at[k], xr_recv.at[k], at_x(k + 1))

    def step(k, _):
        high, low = split(rows[pl.ds(pl.multiple_of(rotate(k, 1, nx) * per_x, per_x), per_x)])
        stream[:, 0:LANES], stream[:, LANES:] = high, low
        left = stream[...]
        total = None
        for j in range(ny * nc * block // tile):
            c = pl.ds(j * tile, tile)
            weight = jnp.exp2(dot(left, prod_hi[c], NT) + dot(left, prod_lo[c], NT))
            slope = dot(left, slope_hi[c], NT) + dot(left, slope_lo[c], NT)
            weighted = weight * slope
            weight_hi, weight_lo = split(weight)
            weighted_hi, weighted_lo = split(weighted)
            term = dot(weighted_hi, mix_w[c], NN) + dot(weighted_lo, mix_w[c], NN)
            term = term + dot(weight_hi, mix_k[c], NN) + dot(weight_lo, mix_k[c], NN)
            total = term if total is None else total + term
        partial[k] = total[:, 0:LANES] + total[:, LANES:]

        @pl.when(k < nx - 1)
        def _():
            x_reduce(k).start()

        return 0

    lax.fori_loop(0, nx, step, 0)

    def z_reduce(d):
        return copy(group.at[d], from_z.at[d], zr_send.at[d], zr_recv.at[d], at_z(d))

    for k in range(nx - 1):
        x_reduce(k).wait_recv()
    for d in sorted(range(nz), key=lambda d: -min(d, nz - d)):
        here = pl.ds(d * block, block)
        total = partial[nx - 1, here]
        for k in range(nx - 1):
            total = total + from_x[k, here]
        group[d] = total
        if d:
            z_reduce(d).start()
    total = group[0]
    for d in range(1, nz):
        z_reduce(d).wait_recv()
        total = total + from_z[d]

    image = jnp.where(lane_b == 0, total, (total - rows[0:block] * total[:, 0:1]) * (1.0 / ROOT))
    pad_p[...] = jnp.zeros_like(pad_p)
    pad_p[0:block] = jnp.where(lane_b <= DESIGN, image, 0.0)
    image = pad_p[...].T
    residual, direction = pad_r[...], pad_d[...]

    def lanes_sum(a):
        return jnp.sum(a, axis=0, keepdims=True)

    sums = [lanes_sum(residual * residual), lanes_sum(direction * image), lanes_sum(residual * image), lanes_sum(image * image)]
    place = lax.broadcasted_iota(jnp.int32, (8, LANES), 0)
    sums = functools.reduce(lambda a, k: jnp.where(place == k, sums[k], a), range(4), jnp.zeros((8, LANES), F32))

    stages = [
        [at_z(d) for d in range(1, nz)],
        [at_cx(c, d) for c in range(nc) for d in range(nx) if c or d],
        [at_y(d) for d in range(1, ny)],
    ]
    for s, targets in enumerate(stages):
        vec[s] = sums
        copies = [
            copy(vec.at[s], vec_in.at[s, i], v_send.at[s, i], v_recv.at[s, i], peer) for i, peer in enumerate(targets)
        ]
        for c in copies:
            c.start()
        for i, c in enumerate(copies):
            c.wait_recv()
            sums = sums + vec_in[s, i]

    sums = jnp.sum(sums, axis=1, keepdims=True)
    norm_old, curvature, cross, square = (sums[k : k + 1] for k in range(4))
    step_size = norm_old / curvature
    norm_new = norm_old - 2.0 * step_size * cross + step_size * step_size * square
    ratio = norm_new / norm_old
    residual_next = residual - step_size * image
    direction_next = residual_next + ratio * direction
    solution_out[...] = solution_ref[...] + step_size * direction_ref[...]
    residual_out[...] = residual_next[0 : DESIGN + 1, 0:block]
    direction_out[...] = direction_next[0 : DESIGN + 1, 0:block]

    for d in range(1, nz):
        z_gather(d).wait_send()
        z_reduce(d).wait_send()
    for d in range(1, ny):
        y_gather(d).wait_send()
    for d in range(1, nx):
        x_gather(d).wait_send()
        x_reduce(d - 1).wait_send()
    for d in range(1, nc):
        c_gather(d).wait_send()
    for s, targets in enumerate(stages):
        for i, peer in enumerate(targets):
            copy(vec.at[s], vec_in.at[s, i], v_send.at[s, i], v_recv.at[s, i], peer).wait_send()


def build(dims, block, tile):
    ny, nc, nz, nx = dims
    width = ny * nc * block
    most = max(nz, ny, nc * nx)
    dma = pltpu.SemaphoreType.DMA
    vmem = pl.BlockSpec(memory_space=pltpu.VMEM)
    state = jax.ShapeDtypeStruct((DESIGN + 1, block), F32)

    def body(points, scales, solution, residual, direction):
        line = jnp.zeros((1, LANES), F32).at[0, 1 : DESIGN + 1].set(scales)
        return pl.pallas_call(
            functools.partial(kernel, dims, block, tile),
            out_shape=(state, state, state),
            in_specs=[vmem] * 5,
            out_specs=(vmem, vmem, vmem),
            scratch_shapes=[
                pltpu.VMEM((LANES, LANES), F32),
                pltpu.VMEM((LANES, LANES), F32),
                pltpu.VMEM((LANES, LANES), F32),
                pltpu.VMEM((nz * nx * block, LANES), F32),
                pltpu.VMEM((nc, ny, 2 * block, LANES), F32),
                pltpu.VMEM((nz * block, 2 * LANES), BF16),
                *[pltpu.VMEM((width, 2 * LANES), BF16) for _ in range(6)],
                pltpu.VMEM((nx, nz * block, LANES), F32),
                pltpu.VMEM((nx - 1, nz * block, LANES), F32),
                pltpu.VMEM((nz, block, LANES), F32),
                pltpu.VMEM((nz, block, LANES), F32),
                pltpu.VMEM((3, 8, LANES), F32),
                pltpu.VMEM((3, most, 8, LANES), F32),
                dma((nz,)), dma((nz,)), dma((nx,)), dma((nx,)), dma((ny,)), dma((ny,)), dma((nc,)), dma((nc,)),
                dma((nx,)), dma((nx,)), dma((nz,)), dma((nz,)), dma((3, most)), dma((3, most)),
            ],
            compiler_params=pltpu.CompilerParams(
                collective_id=0, has_side_effects=True, vmem_limit_bytes=48 * 2**20
            ),
            name="iteration",
        )(points, line, solution, residual, direction)

    return body


def solution(mesh, dims=None, block=80, tile=256):
    if dims is None:
        dims = (mesh.shape["row"] // 2, 2, mesh.shape["col"] // 4, 4)
    state = P(None, ("row", "col"))
    return jax.shard_map(
        build(dims, block, tile),
        mesh=mesh,
        in_specs=(state, P(), state, state, state),
        out_specs=(state, state, state),
        check_vma=False,
    )
```

```python
import functools
import math

import jax
import jax.numpy as jnp
from jax import lax
from jax.experimental import pallas as pl
from jax.experimental.pallas import tpu as pltpu
from jax.sharding import PartitionSpec as P

F32, BF16 = jnp.float32, jnp.bfloat16
MESH = pl.DeviceIdType.MESH
DESIGN = 96
LANES = 128
ROOT = math.sqrt(math.log2(math.e))
NT = (((1,), (1,)), ((), ()))
NN = (((1,), (0,)), ((), ()))
NORM, REST, ONE, ONE2 = 97, 98, 99, 100


def dot(a, b, dims):
    return lax.dot_general(a, b, dims, preferred_element_type=F32)


def split(x):
    high = x.astype(BF16)
    return high, (x - high.astype(F32)).astype(BF16)


def joined(x):
    high, low = split(x)
    return high.astype(F32) + low.astype(F32)


def rotate(index, shift, size):
    return lax.rem(index + shift, size)


def ring(size):
    return sorted(range(size), key=lambda d: (min(d, size - d), d))


def wide(a, b):
    return jnp.concatenate([a, b], axis=1)


def kernel(
    dims, block, tile,
    points_hbm, scales_hbm, solution_hbm, residual_hbm, direction_hbm,
    solution_out, residual_out, direction_out,
    points_ref, scales_ref, solution_ref, residual_ref, direction_ref,
    pad, rows, cols, stream, coord_hi, coord_lo, slope_hi, slope_lo, grad_hi, grad_lo, pipe, acc,
    part, from_core, whole, from_y, vec, vec_in,
    load, z_send, z_recv, x_send, x_recv, y_send, y_recv, c_send, c_recv,
    yr_send, yr_recv, cr_send, cr_recv, v_send, v_recv,
):
    ny, nc, nz, nx = dims
    row, col = lax.axis_index("row"), lax.axis_index("col")
    y, core = row // nc, lax.rem(row, nc)
    z, x = col // nx, lax.rem(col, nx)
    ys, zs, xs = ring(ny), ring(nz), ring(nx)
    per = ny // 2
    half = nc * per * block
    items = 2 * nz * nx * block // tile

    def at_z(shift):
        return (row, rotate(z, shift, nz) * nx + x)

    def at_x(shift):
        return (row, z * nx + rotate(x, shift, nx))

    def at_y(shift):
        return (rotate(y, shift, ny) * nc + core, col)

    def at_cx(dc, dx):
        return (y * nc + rotate(core, dc, nc), z * nx + rotate(x, dx, nx))

    inputs = [
        (points_hbm, points_ref), (scales_hbm, scales_ref), (direction_hbm, direction_ref),
        (residual_hbm, residual_ref), (solution_hbm, solution_ref),
    ]
    loads = [pltpu.make_async_copy(src, dst, load.at[i]) for i, (src, dst) in enumerate(inputs)]
    for c in loads:
        c.start()

    peers = [at_z(d) for d in range(1, nz)] + [at_y(d) for d in range(1, ny)]
    peers += [at_cx(c, d) for c in range(nc) for d in range(nx) if c or d]
    barrier = pltpu.get_barrier_semaphore()
    for peer in peers:
        pl.semaphore_signal(barrier, inc=1, device_id=peer, device_id_type=MESH)

    lane = lax.broadcasted_iota(jnp.int32, (block, LANES), 1)
    for c in loads[:3]:
        c.wait()
    pad[...] = jnp.zeros_like(pad)
    pad[0, :, 1 : DESIGN + 1] = points_ref[...] * (jnp.sqrt(2.0 * scales_ref[...]) * ROOT)
    pad[1, :, 0 : DESIGN + 1] = direction_ref[...]
    coords = joined(pad[0])
    norm = -0.5 * jnp.sum(coords * coords, axis=1, keepdims=True)
    norm_main = joined(norm)
    norm_rest = norm - norm_main
    own_row = jnp.where(lane == NORM, norm_main, coords)
    own_row = jnp.where(lane == REST, norm_rest, own_row)
    own_row = jnp.where((lane == ONE) | (lane == ONE2), 1.0, own_row)
    own_col = jnp.where(lane == ONE, norm_main, coords)
    own_col = jnp.where(lane == ONE2, norm_rest, own_col)
    own_col = jnp.where((lane == NORM) | (lane == REST) | (lane == 0), 1.0, own_col)
    field = pad[1]
    grads = joined(jnp.where(lane >= 1, field * (1.0 / ROOT), 0.0))
    value = field[:, 0:1] - jnp.sum(coords * grads, axis=1, keepdims=True)
    value_main = joined(value)
    own_slope = jnp.where(lane == ONE, value_main, grads)
    own_slope = jnp.where(lane == ONE2, value - value_main, own_slope)
    rows[0, 0, 0:block] = own_row
    cols[0, 0:block] = own_col
    cols[0, block:] = own_slope

    pl.semaphore_wait(barrier, len(peers))

    def copy(src, dst, send, recv, peer):
        return pltpu.make_async_remote_copy(
            src_ref=src, dst_ref=dst, send_sem=send, recv_sem=recv, device_id=peer, device_id_type=MESH
        )

    def y_gather(r):
        h, k = divmod(r, per)
        there = rows.at[h, 0, pl.ds(k * block, block)]
        return copy(rows.at[0, 0, pl.ds(0, block)], there, y_send.at[r], y_recv.at[r], at_y(ny - ys[r]))

    def c_gather(h):
        return copy(rows.at[h, 0], rows.at[h, 1], c_send.at[h], c_recv.at[h], at_cx(1, 0))

    def z_gather(r):
        return copy(cols.at[0], cols.at[r * nx], z_send.at[r], z_recv.at[r], at_z(nz - zs[r]))

    def x_gather(r, i):
        here, there = cols.at[r * nx], cols.at[r * nx + i]
        return copy(here, there, x_send.at[r * nx + i], x_recv.at[r * nx + i], at_x(nx - xs[i]))

    def pass_on(r):
        if r:
            z_gather(r).wait_recv()
        for i in range(1, nx):
            x_gather(r, i).start()

    for r in range(1, max(ny, nz)):
        if r < ny:
            y_gather(r).start()
        if r < nz:
            z_gather(r).start()
        if r == 1:
            pass_on(0)
    acc[...] = jnp.zeros_like(acc)
    for c in loads[3:]:
        c.wait()
    residual, direction = residual_ref[...], direction_ref[...]

    def total_of(a):
        return jnp.sum(jnp.sum(a, axis=1, keepdims=True), axis=0, keepdims=True)

    norm_old = total_of(residual * residual)

    def factor(s, _):
        @pl.when(lax.rem(s, nx) > 0)
        def _():
            copy(cols.at[0], cols.at[s], x_send.at[s], x_recv.at[s], at_x(1)).wait_recv()

        here = pl.ds(pl.multiple_of(s * block, block), block)
        slope = cols[s, block:]
        coord_hi[here], coord_lo[here] = split(cols[s, 0:block])
        slope_hi[here], slope_lo[here] = split(slope)
        grad_hi[here], grad_lo[here] = split(slope * (ROOT * ROOT))
        return 0

    def rows_in(h):
        for r in range(h * per, (h + 1) * per):
            if r:
                y_gather(r).wait_recv()
        c_gather(h).start()
        c_gather(h).wait_recv()
        for c in range(nc):
            here = pl.ds(c * per * block, per * block)
            stream[h, here, 0:LANES], stream[h, here, LANES:] = split(rows[h, c])

    def place(n):
        def since(c):
            return (n + items - c) // items

        pair = since(2) - since(items // 2)
        far = since(items // 2) - since(4 * items // 5)
        last = since(4 * items // 5)
        h = pair * lax.rem(n, 2) + far
        t = (1 - since(2)) * n + pair * (n // 2 + 1 - 2 * lax.rem(n, 2))
        t = t + far * (n - 3 * items // 10) + last * (n - items // 2)
        fresh = (1 - h) * (1 - since(items // 2)) + since(3 * items // 5) - last
        return h, t, fresh

    def columns(t):
        return pl.ds(pl.multiple_of(t * tile, tile), tile)

    def first(n):
        h, t, fresh = place(n)
        low = (t * tile + block - 1) // block
        high = ((t + 1) * tile + block - 1) // block
        lax.fori_loop(low, low + fresh * (high - low), factor, 0)
        c, left = columns(t), stream[h]
        chi, clo, shi, slo = coord_hi[c], coord_lo[c], slope_hi[c], slope_lo[c]
        weight = jnp.exp2(dot(left, wide(chi, chi), NT) + dot(left, wide(clo, clo), NT))
        weighted = weight * (dot(left, wide(shi, shi), NT) + dot(left, wide(slo, slo), NT))
        return (*split(weighted), *split(weight))

    def second(n):
        h, t, _ = place(n)
        c, slot = columns(t), lax.rem(n, 2)
        by_coord, by_grad = wide(coord_hi[c], coord_lo[c]), wide(grad_hi[c], grad_lo[c])
        term = dot(pipe[slot, 0], by_coord, NN) + dot(pipe[slot, 1], by_coord, NN)
        term = term + dot(pipe[slot, 2], by_grad, NN) + dot(pipe[slot, 3], by_grad, NN)
        acc[h] = acc[h] + term

    def keep(n, values):
        slot = lax.rem(n, 2)
        for i, value in enumerate(values):
            pipe[slot, i] = value

    def c_reduce(h):
        return copy(part.at[h, 1], from_core.at[h], cr_send.at[h], cr_recv.at[h], at_cx(1, 0))

    def y_reduce(r):
        h, k = divmod(r, per)
        return copy(whole.at[h, pl.ds(k * block, block)], from_y.at[r], yr_send.at[r], yr_recv.at[r], at_y(ys[r]))

    def to_core(h):
        for c in range(nc):
            here = pl.ds(c * per * block, per * block)
            part[h, c] = acc[h, here, 0:LANES] + acc[h, here, LANES:]
        c_reduce(h).start()

    def to_y(h):
        c_reduce(h).wait_recv()
        whole[h] = part[h, 0] + from_core[h]
        for r in reversed(range(h * per, (h + 1) * per)):
            if r:
                y_reduce(r).start()

    def body(n, _):
        for at, ranks in events.items():

            @pl.when(n == at)
            def _(ranks=ranks):
                for r in ranks:
                    pass_on(r)

        @pl.when(n == 2)
        def _():
            rows_in(1)

        @pl.when(n == 4 * items // 5)
        def _():
            to_core(1)

        @pl.when(n == 4 * items // 5 + 1)
        def _():
            to_y(1)

        values = first(n + 1)
        second(n)
        keep(n + 1, values)
        return 0

    early = [r for r in (1, 2) if r < nz]
    events = {at: [r for r in ranks if r < nz] for at, ranks in EVENTS.items()}
    for r in early:
        pass_on(r)
    rows_in(0)
    keep(0, first(0))
    lax.fori_loop(0, items - 1, body, 0)
    second(items - 1)
    to_core(0)
    to_y(0)

    total = whole[0, 0:block]
    for r in range(1, ny):
        y_reduce(r).wait_recv()
        total = total + from_y[r]
    image = jnp.where(lane == 0, total, (total - own_row * total[:, 0:1]) * (1.0 / ROOT))[:, 0 : DESIGN + 1]

    sums = [norm_old, total_of(direction * image), total_of(residual * image), total_of(image * image)]
    spot = lax.broadcasted_iota(jnp.int32, (1, LANES), 1)
    line = jnp.zeros((1, LANES), F32)
    for k, value in enumerate(sums):
        line = jnp.where(spot == k, value, line)

    stages = [
        [at_z(d) for d in range(1, nz)],
        [at_cx(c, d) for c in range(nc) for d in range(nx) if c or d],
        [at_y(d) for d in range(1, ny)],
    ]
    exchanges = [
        [copy(vec.at[s], vec_in.at[s, i], v_send.at[s, i], v_recv.at[s, i], peer) for i, peer in enumerate(targets)]
        for s, targets in enumerate(stages)
    ]
    for s, copies in enumerate(exchanges):
        vec[s] = line
        for c in copies:
            c.start()
        for i, c in enumerate(copies):
            c.wait_recv()
            line = line + vec_in[s, i]

    norm_old, curvature, cross, square = (line[:, k : k + 1] for k in range(4))
    step_size = norm_old / curvature
    norm_new = norm_old - 2.0 * step_size * cross + step_size * step_size * square
    residual_next = residual - step_size * image
    solution_out[...] = solution_ref[...] + step_size * direction
    residual_out[...] = residual_next
    direction_out[...] = residual_next + norm_new / norm_old * direction

    for r in range(1, nz):
        z_gather(r).wait_send()
    for r in range(nz):
        for i in range(1, nx):
            x_gather(r, i).wait_send()
    for r in range(1, ny):
        y_gather(r).wait_send()
        y_reduce(r).wait_send()
    for h in range(2):
        c_gather(h).wait_send()
        c_reduce(h).wait_send()
    for copies in exchanges:
        for c in copies:
            c.wait_send()


EVENTS = {1: (3, 4), 6: (5, 6), 9: (7,)}


def build(dims, block, tile):
    ny, nc, nz, nx = dims
    width = nz * nx * block
    half = nc * ny * block // 2
    most = max(nz, ny, nc * nx)
    dma = pltpu.SemaphoreType.DMA
    vmem, hbm = pl.BlockSpec(memory_space=pltpu.VMEM), pl.BlockSpec(memory_space=pltpu.HBM)
    state = jax.ShapeDtypeStruct((block, DESIGN + 1), F32)
    inputs = [(block, DESIGN), (1, DESIGN)] + [(block, DESIGN + 1)] * 3

    def body(points, scales, solution, residual, direction):
        outs = pl.pallas_call(
            functools.partial(kernel, dims, block, tile),
            out_shape=(state, state, state),
            in_specs=[hbm] * 5,
            out_specs=(vmem, vmem, vmem),
            scratch_shapes=[
                *[pltpu.VMEM(shape, F32) for shape in inputs],
                pltpu.VMEM((2, block, LANES), F32),
                pltpu.VMEM((2, nc, ny // 2 * block, LANES), F32),
                pltpu.VMEM((nz * nx, 2 * block, LANES), F32),
                pltpu.VMEM((2, half, 2 * LANES), BF16),
                *[pltpu.VMEM((width, LANES), BF16) for _ in range(6)],
                pltpu.VMEM((2, 4, half, tile), BF16),
                pltpu.VMEM((2, half, 2 * LANES), F32),
                pltpu.VMEM((2, nc, ny // 2 * block, LANES), F32),
                pltpu.VMEM((2, ny // 2 * block, LANES), F32),
                pltpu.VMEM((2, ny // 2 * block, LANES), F32),
                pltpu.VMEM((ny, block, LANES), F32),
                pltpu.VMEM((3, 1, LANES), F32),
                pltpu.VMEM((3, most, 1, LANES), F32),
                dma((5,)), dma((nz,)), dma((nz,)), dma((nz * nx,)), dma((nz * nx,)), dma((ny,)), dma((ny,)),
                dma((2,)), dma((2,)), dma((ny,)), dma((ny,)), dma((2,)), dma((2,)), dma((3, most)), dma((3, most)),
            ],
            compiler_params=pltpu.CompilerParams(
                collective_id=0, has_side_effects=True, vmem_limit_bytes=48 * 2**20
            ),
            name="iteration",
        )(points.T, scales.reshape(1, DESIGN), solution.T, residual.T, direction.T)
        return tuple(o.T for o in outs)

    return body


def solution(mesh, dims=None, block=80, tile=256):
    if dims is None:
        dims = (mesh.shape["row"] // 2, 2, mesh.shape["col"] // 4, 4)
    state = P(None, ("row", "col"))
    return jax.shard_map(
        build(dims, block, tile),
        mesh=mesh,
        in_specs=(state, P(), state, state, state),
        out_specs=(state, state, state),
        check_vma=False,
    )
```

```python
import functools
import math

import jax
import jax.numpy as jnp
from jax import lax
from jax.experimental import pallas as pl
from jax.experimental.pallas import tpu as pltpu
from jax.sharding import PartitionSpec as P

F32, BF16 = jnp.float32, jnp.bfloat16
MESH = pl.DeviceIdType.MESH
DESIGN = 96
LANES = 128
ROOT = math.sqrt(math.log2(math.e))
NT = (((1,), (1,)), ((), ()))
NN = (((1,), (0,)), ((), ()))
NORM, REST, ONE, ONE2 = 97, 98, 99, 100


def dot(a, b, dims):
    return lax.dot_general(a, b, dims, preferred_element_type=F32)


def split(x):
    high = x.astype(BF16)
    return high, (x - high.astype(F32)).astype(BF16)


def joined(x):
    high, low = split(x)
    return high.astype(F32) + low.astype(F32)


def rotate(index, shift, size):
    return lax.rem(index + shift, size)


def ring(size):
    return sorted(range(size), key=lambda d: (min(d, size - d), d))


def wide(a, b):
    return jnp.concatenate([a, b], axis=1)


def kernel(
    dims, block, tile,
    points_hbm, scales_hbm, solution_hbm, residual_hbm, direction_hbm,
    solution_out, residual_out, direction_out,
    points_ref, scales_ref, solution_ref, residual_ref, direction_ref,
    pad, rows, cols, stream, coord_hi, coord_lo, slope_hi, slope_lo, grad_hi, grad_lo, pipe, acc,
    part, from_core, whole, from_y, vec, vec_in,
    load, z_send, z_recv, x_send, x_recv, y_send, y_recv, c_send, c_recv,
    yr_send, yr_recv, cr_send, cr_recv, v_send, v_recv,
):
    ny, nc, nz, nx = dims
    row, col = lax.axis_index("row"), lax.axis_index("col")
    y, core = row // nc, lax.rem(row, nc)
    z, x = col // nx, lax.rem(col, nx)
    ys, zs, xs = ring(ny), ring(nz), ring(nx)
    per = ny // 2
    half = nc * per * block
    items = 2 * nz * nx * block // tile

    def at_z(shift):
        return (row, rotate(z, shift, nz) * nx + x)

    def at_x(shift):
        return (row, z * nx + rotate(x, shift, nx))

    def at_y(shift):
        return (rotate(y, shift, ny) * nc + core, col)

    def at_cx(dc, dx):
        return (y * nc + rotate(core, dc, nc), z * nx + rotate(x, dx, nx))

    inputs = [
        (points_hbm, points_ref), (scales_hbm, scales_ref), (direction_hbm, direction_ref),
        (residual_hbm, residual_ref), (solution_hbm, solution_ref),
    ]
    loads = [pltpu.make_async_copy(src, dst, load.at[i]) for i, (src, dst) in enumerate(inputs)]
    for c in loads:
        c.start()

    peers = [at_z(d) for d in range(1, nz)] + [at_y(d) for d in range(1, ny)]
    peers += [at_cx(c, d) for c in range(nc) for d in range(nx) if c or d]
    barrier = pltpu.get_barrier_semaphore()
    for peer in peers:
        pl.semaphore_signal(barrier, inc=1, device_id=peer, device_id_type=MESH)

    lane = lax.broadcasted_iota(jnp.int32, (block, LANES), 1)
    for c in loads[:3]:
        c.wait()
    pad[...] = jnp.zeros_like(pad)
    pad[0, :, 1 : DESIGN + 1] = points_ref[...] * (jnp.sqrt(2.0 * scales_ref[...]) * ROOT)
    pad[1, :, 0 : DESIGN + 1] = direction_ref[...]
    coords = joined(pad[0])
    norm = -0.5 * jnp.sum(coords * coords, axis=1, keepdims=True)
    norm_main = joined(norm)
    norm_rest = norm - norm_main
    own_row = jnp.where(lane == NORM, norm_main, coords)
    own_row = jnp.where(lane == REST, norm_rest, own_row)
    own_row = jnp.where((lane == ONE) | (lane == ONE2), 1.0, own_row)
    own_col = jnp.where(lane == ONE, norm_main, coords)
    own_col = jnp.where(lane == ONE2, norm_rest, own_col)
    own_col = jnp.where((lane == NORM) | (lane == REST) | (lane == 0), 1.0, own_col)
    field = pad[1]
    grads = joined(jnp.where(lane >= 1, field * (1.0 / ROOT), 0.0))
    value = field[:, 0:1] - jnp.sum(coords * grads, axis=1, keepdims=True)
    value_main = joined(value)
    own_slope = jnp.where(lane == ONE, value_main, grads)
    own_slope = jnp.where(lane == ONE2, value - value_main, own_slope)
    rows[0, 0, 0:block] = own_row
    cols[0, 0:block] = own_col
    cols[0, block:] = own_slope

    pl.semaphore_wait(barrier, len(peers))

    def copy(src, dst, send, recv, peer):
        return pltpu.make_async_remote_copy(
            src_ref=src, dst_ref=dst, send_sem=send, recv_sem=recv, device_id=peer, device_id_type=MESH
        )

    def y_gather(r):
        h, k = divmod(r, per)
        there = rows.at[h, 0, pl.ds(k * block, block)]
        return copy(rows.at[0, 0, pl.ds(0, block)], there, y_send.at[r], y_recv.at[r], at_y(ny - ys[r]))

    def c_gather(h):
        return copy(rows.at[h, 0], rows.at[h, 1], c_send.at[h], c_recv.at[h], at_cx(1, 0))

    def z_gather(r):
        return copy(cols.at[0], cols.at[r * nx], z_send.at[r], z_recv.at[r], at_z(nz - zs[r]))

    def x_gather(r, i):
        here, there = cols.at[r * nx], cols.at[r * nx + i]
        return copy(here, there, x_send.at[r * nx + i], x_recv.at[r * nx + i], at_x(nx - xs[i]))

    def pass_on(r):
        if r:
            z_gather(r).wait_recv()
        for i in range(1, nx):
            x_gather(r, i).start()

    for r in range(1, max(ny, nz)):
        if r < ny:
            y_gather(r).start()
        if r < nz:
            z_gather(r).start()
        if r == 1:
            pass_on(0)
    acc[...] = jnp.zeros_like(acc)
    for c in loads[3:]:
        c.wait()
    residual, direction = residual_ref[...], direction_ref[...]

    def total_of(a):
        return jnp.sum(jnp.sum(a, axis=1, keepdims=True), axis=0, keepdims=True)

    norm_old = total_of(residual * residual)

    def factor(s, _):
        @pl.when(lax.rem(s, nx) > 0)
        def _():
            copy(cols.at[0], cols.at[s], x_send.at[s], x_recv.at[s], at_x(1)).wait_recv()

        here = pl.ds(pl.multiple_of(s * block, block), block)
        slope = cols[s, block:]
        coord_hi[here], coord_lo[here] = split(cols[s, 0:block])
        slope_hi[here], slope_lo[here] = split(slope)
        grad_hi[here], grad_lo[here] = split(slope * (ROOT * ROOT))
        return 0

    def rows_in(h):
        for r in range(h * per, (h + 1) * per):
            if r:
                y_gather(r).wait_recv()
        c_gather(h).start()
        c_gather(h).wait_recv()
        for c in range(nc):
            here = pl.ds(c * per * block, per * block)
            stream[h, here, 0:LANES], stream[h, here, LANES:] = split(rows[h, c])

    def place(n):
        def since(c):
            return (n + items - c) // items

        pair = since(2) - since(2 + 2 * PAIRS)
        last = since(2 + PAIRS + items // 2)
        far = since(2 + 2 * PAIRS) - last
        h = pair * lax.rem(n, 2) + far
        t = (1 - since(2)) * n + pair * (n // 2 + 1 - 2 * lax.rem(n, 2))
        t = t + far * (n - 2 - PAIRS) + last * (n - items // 2)
        fresh = (1 - h) * (1 - last) + since(4 + 2 * PAIRS) - last
        return h, t, fresh

    def columns(t):
        return pl.ds(pl.multiple_of(t * tile, tile), tile)

    def first(n):
        h, t, fresh = place(n)
        low = (t * tile + block - 1) // block
        high = ((t + 1) * tile + block - 1) // block
        lax.fori_loop(low, low + fresh * (high - low), factor, 0)
        c, left = columns(t), stream[h]
        chi, clo, shi, slo = coord_hi[c], coord_lo[c], slope_hi[c], slope_lo[c]
        weight = jnp.exp2(dot(left, wide(chi, chi), NT) + dot(left, wide(clo, clo), NT))
        weighted = weight * (dot(left, wide(shi, shi), NT) + dot(left, wide(slo, slo), NT))
        return (*split(weighted), *split(weight))

    def second(n):
        h, t, _ = place(n)
        c, slot = columns(t), lax.rem(n, 2)
        by_coord, by_grad = wide(coord_hi[c], coord_lo[c]), wide(grad_hi[c], grad_lo[c])
        term = dot(pipe[slot, 0], by_coord, NN) + dot(pipe[slot, 1], by_coord, NN)
        term = term + dot(pipe[slot, 2], by_grad, NN) + dot(pipe[slot, 3], by_grad, NN)
        acc[h] = acc[h] + term

    def keep(n, values):
        slot = lax.rem(n, 2)
        for i, value in enumerate(values):
            pipe[slot, i] = value

    def c_reduce(h):
        return copy(part.at[h, 1], from_core.at[h], cr_send.at[h], cr_recv.at[h], at_cx(1, 0))

    def y_reduce(r):
        h, k = divmod(r, per)
        return copy(whole.at[h, pl.ds(k * block, block)], from_y.at[r], yr_send.at[r], yr_recv.at[r], at_y(ys[r]))

    def to_core(h):
        for c in range(nc):
            here = pl.ds(c * per * block, per * block)
            part[h, c] = acc[h, here, 0:LANES] + acc[h, here, LANES:]
        c_reduce(h).start()

    def to_y(h):
        c_reduce(h).wait_recv()
        whole[h] = part[h, 0] + from_core[h]
        for r in reversed(range(h * per, (h + 1) * per)):
            if r:
                y_reduce(r).start()

    def body(n, _):
        for at, ranks in events.items():

            @pl.when(n == at)
            def _(ranks=ranks):
                for r in ranks:
                    pass_on(r)

        @pl.when(n == 2)
        def _():
            rows_in(1)

        @pl.when(n == 2 + PAIRS + items // 2)
        def _():
            to_core(1)

        @pl.when(n == 3 + PAIRS + items // 2)
        def _():
            to_y(1)

        values = first(n + 1)
        second(n)
        keep(n + 1, values)
        return 0

    early = [r for r in (1, 2) if r < nz]
    events = {at: [r for r in ranks if r < nz] for at, ranks in EVENTS.items()}
    for r in early:
        pass_on(r)
    rows_in(0)
    keep(0, first(0))
    lax.fori_loop(0, items - 1, body, 0)
    second(items - 1)
    to_core(0)
    to_y(0)

    total = whole[0, 0:block]
    for r in range(1, ny):
        y_reduce(r).wait_recv()
        total = total + from_y[r]
    image = jnp.where(lane == 0, total, (total - own_row * total[:, 0:1]) * (1.0 / ROOT))[:, 0 : DESIGN + 1]

    sums = [norm_old, total_of(direction * image), total_of(residual * image), total_of(image * image)]
    spot = lax.broadcasted_iota(jnp.int32, (1, LANES), 1)
    line = jnp.zeros((1, LANES), F32)
    for k, value in enumerate(sums):
        line = jnp.where(spot == k, value, line)

    stages = [
        [at_z(d) for d in range(1, nz)],
        [at_cx(c, d) for c in range(nc) for d in range(nx) if c or d],
        [at_y(d) for d in range(1, ny)],
    ]
    exchanges = [
        [copy(vec.at[s], vec_in.at[s, i], v_send.at[s, i], v_recv.at[s, i], peer) for i, peer in enumerate(targets)]
        for s, targets in enumerate(stages)
    ]
    for s, copies in enumerate(exchanges):
        vec[s] = line
        for c in copies:
            c.start()
        for i, c in enumerate(copies):
            c.wait_recv()
            line = line + vec_in[s, i]

    norm_old, curvature, cross, square = (line[:, k : k + 1] for k in range(4))
    step_size = norm_old / curvature
    norm_new = norm_old - 2.0 * step_size * cross + step_size * step_size * square
    residual_next = residual - step_size * image
    solution_out[...] = solution_ref[...] + step_size * direction
    residual_out[...] = residual_next
    direction_out[...] = residual_next + norm_new / norm_old * direction

    for r in range(1, nz):
        z_gather(r).wait_send()
    for r in range(nz):
        for i in range(1, nx):
            x_gather(r, i).wait_send()
    for r in range(1, ny):
        y_gather(r).wait_send()
        y_reduce(r).wait_send()
    for h in range(2):
        c_gather(h).wait_send()
        c_reduce(h).wait_send()
    for copies in exchanges:
        for c in copies:
            c.wait_send()


EVENTS = {0: (3,), 1: (4,), 3: (5,), 4: (6,), 6: (7,)}

PAIRS = 4


def build(dims, block, tile):
    ny, nc, nz, nx = dims
    width = nz * nx * block
    half = nc * ny * block // 2
    most = max(nz, ny, nc * nx)
    dma = pltpu.SemaphoreType.DMA
    vmem, hbm = pl.BlockSpec(memory_space=pltpu.VMEM), pl.BlockSpec(memory_space=pltpu.HBM)
    state = jax.ShapeDtypeStruct((block, DESIGN + 1), F32)
    inputs = [(block, DESIGN), (1, DESIGN)] + [(block, DESIGN + 1)] * 3

    def body(points, scales, solution, residual, direction):
        outs = pl.pallas_call(
            functools.partial(kernel, dims, block, tile),
            out_shape=(state, state, state),
            in_specs=[hbm] * 5,
            out_specs=(vmem, vmem, vmem),
            scratch_shapes=[
                *[pltpu.VMEM(shape, F32) for shape in inputs],
                pltpu.VMEM((2, block, LANES), F32),
                pltpu.VMEM((2, nc, ny // 2 * block, LANES), F32),
                pltpu.VMEM((nz * nx, 2 * block, LANES), F32),
                pltpu.VMEM((2, half, 2 * LANES), BF16),
                *[pltpu.VMEM((width, LANES), BF16) for _ in range(6)],
                pltpu.VMEM((2, 4, half, tile), BF16),
                pltpu.VMEM((2, half, 2 * LANES), F32),
                pltpu.VMEM((2, nc, ny // 2 * block, LANES), F32),
                pltpu.VMEM((2, ny // 2 * block, LANES), F32),
                pltpu.VMEM((2, ny // 2 * block, LANES), F32),
                pltpu.VMEM((ny, block, LANES), F32),
                pltpu.VMEM((3, 1, LANES), F32),
                pltpu.VMEM((3, most, 1, LANES), F32),
                dma((5,)), dma((nz,)), dma((nz,)), dma((nz * nx,)), dma((nz * nx,)), dma((ny,)), dma((ny,)),
                dma((2,)), dma((2,)), dma((ny,)), dma((ny,)), dma((2,)), dma((2,)), dma((3, most)), dma((3, most)),
            ],
            compiler_params=pltpu.CompilerParams(
                collective_id=0, has_side_effects=True, vmem_limit_bytes=60 * 2**20
            ),
            name="iteration",
        )(points.T, scales.reshape(1, DESIGN), solution.T, residual.T, direction.T)
        return tuple(o.T for o in outs)

    return body


def solution(mesh, dims=None, block=80, tile=256):
    if dims is None:
        dims = (mesh.shape["row"] // 2, 2, mesh.shape["col"] // 4, 4)
    state = P(None, ("row", "col"))
    return jax.shard_map(
        build(dims, block, tile),
        mesh=mesh,
        in_specs=(state, P(), state, state, state),
        out_specs=(state, state, state),
        check_vma=False,
    )
```

```python
import functools
import math

import jax
import jax.numpy as jnp
from jax import lax
from jax.experimental import pallas as pl
from jax.experimental.pallas import tpu as pltpu
from jax.sharding import PartitionSpec as P

F32, BF16 = jnp.float32, jnp.bfloat16
MESH = pl.DeviceIdType.MESH
DESIGN = 96
LANES = 128
ROOT = math.sqrt(math.log2(math.e))
NT = (((1,), (1,)), ((), ()))
NN = (((1,), (0,)), ((), ()))
NORM, REST, ONE, ONE2 = 97, 98, 99, 100


def dot(a, b, dims):
    return lax.dot_general(a, b, dims, preferred_element_type=F32)


def split(x):
    high = x.astype(BF16)
    return high, (x - high.astype(F32)).astype(BF16)


def joined(x):
    high, low = split(x)
    return high.astype(F32) + low.astype(F32)


def rotate(index, shift, size):
    return lax.rem(index + shift, size)


def ring(size):
    return sorted(range(size), key=lambda d: (min(d, size - d), d))


def wide(a, b):
    return jnp.concatenate([a, b], axis=1)


def kernel(
    dims, block, tile,
    points_hbm, scales_hbm, residual_hbm, direction_hbm,
    image_out, sums_out,
    points_ref, scales_ref, residual_ref, direction_ref,
    pad, rows, cols, stream, coord_hi, coord_lo, slope_hi, slope_lo, grad_hi, grad_lo, pipe, acc,
    part, from_core, whole, from_y, vec, vec_in,
    load, z_send, z_recv, x_send, x_recv, y_send, y_recv, c_send, c_recv,
    yr_send, yr_recv, cr_send, cr_recv, v_send, v_recv,
):
    ny, nc, nz, nx = dims
    row, col = lax.axis_index("row"), lax.axis_index("col")
    y, core = row // nc, lax.rem(row, nc)
    z, x = col // nx, lax.rem(col, nx)
    ys, zs, xs = ring(ny), ring(nz), ring(nx)
    per = ny // 2
    half = nc * per * block
    items = 2 * nz * nx * block // tile

    def at_z(shift):
        return (row, rotate(z, shift, nz) * nx + x)

    def at_x(shift):
        return (row, z * nx + rotate(x, shift, nx))

    def at_y(shift):
        return (rotate(y, shift, ny) * nc + core, col)

    def at_cx(dc, dx):
        return (y * nc + rotate(core, dc, nc), z * nx + rotate(x, dx, nx))

    inputs = [
        (points_hbm, points_ref), (scales_hbm, scales_ref), (direction_hbm, direction_ref),
        (residual_hbm, residual_ref),
    ]
    loads = [pltpu.make_async_copy(src, dst, load.at[i]) for i, (src, dst) in enumerate(inputs)]
    for c in loads:
        c.start()

    peers = [at_z(d) for d in range(1, nz)] + [at_y(d) for d in range(1, ny)]
    peers += [at_cx(c, d) for c in range(nc) for d in range(nx) if c or d]
    barrier = pltpu.get_barrier_semaphore()
    for peer in peers:
        pl.semaphore_signal(barrier, inc=1, device_id=peer, device_id_type=MESH)

    lane = lax.broadcasted_iota(jnp.int32, (block, LANES), 1)
    for c in loads[:3]:
        c.wait()
    pad[...] = jnp.zeros_like(pad)
    pad[0, :, 1 : DESIGN + 1] = points_ref[...] * (jnp.sqrt(2.0 * scales_ref[...]) * ROOT)
    pad[1, :, 0 : DESIGN + 1] = direction_ref[...]
    coords = joined(pad[0])
    norm = -0.5 * jnp.sum(coords * coords, axis=1, keepdims=True)
    norm_main = joined(norm)
    norm_rest = norm - norm_main
    own_row = jnp.where(lane == NORM, norm_main, coords)
    own_row = jnp.where(lane == REST, norm_rest, own_row)
    own_row = jnp.where((lane == ONE) | (lane == ONE2), 1.0, own_row)
    own_col = jnp.where(lane == ONE, norm_main, coords)
    own_col = jnp.where(lane == ONE2, norm_rest, own_col)
    own_col = jnp.where((lane == NORM) | (lane == REST) | (lane == 0), 1.0, own_col)
    field = pad[1]
    grads = joined(jnp.where(lane >= 1, field * (1.0 / ROOT), 0.0))
    value = field[:, 0:1] - jnp.sum(coords * grads, axis=1, keepdims=True)
    value_main = joined(value)
    own_slope = jnp.where(lane == ONE, value_main, grads)
    own_slope = jnp.where(lane == ONE2, value - value_main, own_slope)
    rows[0, 0, 0:block] = own_row
    cols[0, 0:block] = own_col
    cols[0, block:] = own_slope

    pl.semaphore_wait(barrier, len(peers))

    def copy(src, dst, send, recv, peer):
        return pltpu.make_async_remote_copy(
            src_ref=src, dst_ref=dst, send_sem=send, recv_sem=recv, device_id=peer, device_id_type=MESH
        )

    def y_gather(r):
        h, k = divmod(r, per)
        there = rows.at[h, 0, pl.ds(k * block, block)]
        return copy(rows.at[0, 0, pl.ds(0, block)], there, y_send.at[r], y_recv.at[r], at_y(ny - ys[r]))

    def c_gather(h):
        return copy(rows.at[h, 0], rows.at[h, 1], c_send.at[h], c_recv.at[h], at_cx(1, 0))

    def z_gather(r):
        return copy(cols.at[0], cols.at[r * nx], z_send.at[r], z_recv.at[r], at_z(nz - zs[r]))

    def x_gather(r, i):
        here, there = cols.at[r * nx], cols.at[r * nx + i]
        return copy(here, there, x_send.at[r * nx + i], x_recv.at[r * nx + i], at_x(nx - xs[i]))

    def pass_on(r):
        if r:
            z_gather(r).wait_recv()
        for i in range(1, nx):
            x_gather(r, i).start()

    for r in range(1, max(ny, nz)):
        if r < ny:
            y_gather(r).start()
        if r < nz:
            z_gather(r).start()
        if r == 1:
            pass_on(0)
    acc[...] = jnp.zeros_like(acc)
    for c in loads[3:]:
        c.wait()
    residual, direction = residual_ref[...], direction_ref[...]

    def total_of(a):
        return jnp.sum(jnp.sum(a, axis=1, keepdims=True), axis=0, keepdims=True)

    norm_old = total_of(residual * residual)

    def factor(s, _):
        @pl.when(lax.rem(s, nx) > 0)
        def _():
            copy(cols.at[0], cols.at[s], x_send.at[s], x_recv.at[s], at_x(1)).wait_recv()

        here = pl.ds(pl.multiple_of(s * block, block), block)
        slope = cols[s, block:]
        coord_hi[here], coord_lo[here] = split(cols[s, 0:block])
        slope_hi[here], slope_lo[here] = split(slope)
        grad_hi[here], grad_lo[here] = split(slope * (ROOT * ROOT))
        return 0

    def rows_in(h):
        for r in range(h * per, (h + 1) * per):
            if r:
                y_gather(r).wait_recv()
        c_gather(h).start()
        c_gather(h).wait_recv()
        for c in range(nc):
            here = pl.ds(c * per * block, per * block)
            stream[h, here, 0:LANES], stream[h, here, LANES:] = split(rows[h, c])

    def place(n):
        def since(c):
            return (n + items - c) // items

        pair = since(2) - since(2 + 2 * PAIRS)
        last = since(2 + PAIRS + items // 2)
        far = since(2 + 2 * PAIRS) - last
        h = pair * lax.rem(n, 2) + far
        t = (1 - since(2)) * n + pair * (n // 2 + 1 - 2 * lax.rem(n, 2))
        t = t + far * (n - 2 - PAIRS) + last * (n - items // 2)
        fresh = (1 - h) * (1 - last) + since(4 + 2 * PAIRS) - last
        return h, t, fresh

    def columns(t):
        return pl.ds(pl.multiple_of(t * tile, tile), tile)

    def first(n):
        h, t, fresh = place(n)
        low = (t * tile + block - 1) // block
        high = ((t + 1) * tile + block - 1) // block
        lax.fori_loop(low, low + fresh * (high - low), factor, 0)
        c, left = columns(t), stream[h]
        chi, clo, shi, slo = coord_hi[c], coord_lo[c], slope_hi[c], slope_lo[c]
        weight = jnp.exp2(dot(left, wide(chi, chi), NT) + dot(left, wide(clo, clo), NT))
        weighted = weight * (dot(left, wide(shi, shi), NT) + dot(left, wide(slo, slo), NT))
        return (*split(weighted), *split(weight))

    def second(n):
        h, t, _ = place(n)
        c, slot = columns(t), lax.rem(n, 2)
        by_coord, by_grad = wide(coord_hi[c], coord_lo[c]), wide(grad_hi[c], grad_lo[c])
        term = dot(pipe[slot, 0], by_coord, NN) + dot(pipe[slot, 1], by_coord, NN)
        term = term + dot(pipe[slot, 2], by_grad, NN) + dot(pipe[slot, 3], by_grad, NN)
        acc[h] = acc[h] + term

    def keep(n, values):
        slot = lax.rem(n, 2)
        for i, value in enumerate(values):
            pipe[slot, i] = value

    def c_reduce(h):
        return copy(part.at[h, 1], from_core.at[h], cr_send.at[h], cr_recv.at[h], at_cx(1, 0))

    def y_reduce(r):
        h, k = divmod(r, per)
        return copy(whole.at[h, pl.ds(k * block, block)], from_y.at[r], yr_send.at[r], yr_recv.at[r], at_y(ys[r]))

    def to_core(h):
        for c in range(nc):
            here = pl.ds(c * per * block, per * block)
            part[h, c] = acc[h, here, 0:LANES] + acc[h, here, LANES:]
        c_reduce(h).start()

    def to_y(h):
        c_reduce(h).wait_recv()
        whole[h] = part[h, 0] + from_core[h]
        for r in reversed(range(h * per, (h + 1) * per)):
            if r:
                y_reduce(r).start()

    def body(n, _):
        for at, ranks in events.items():

            @pl.when(n == at)
            def _(ranks=ranks):
                for r in ranks:
                    pass_on(r)

        @pl.when(n == 2)
        def _():
            rows_in(1)

        @pl.when(n == 2 + PAIRS + items // 2)
        def _():
            to_core(1)

        @pl.when(n == 3 + PAIRS + items // 2)
        def _():
            to_y(1)

        values = first(n + 1)
        second(n)
        keep(n + 1, values)
        return 0

    early = [r for r in (1, 2) if r < nz]
    events = {at: [r for r in ranks if r < nz] for at, ranks in EVENTS.items()}
    for r in early:
        pass_on(r)
    rows_in(0)
    keep(0, first(0))
    lax.fori_loop(0, items - 1, body, 0)
    second(items - 1)
    to_core(0)
    to_y(0)

    total = whole[0, 0:block]
    for r in range(1, ny):
        y_reduce(r).wait_recv()
        total = total + from_y[r]
    image = jnp.where(lane == 0, total, (total - own_row * total[:, 0:1]) * (1.0 / ROOT))[:, 0 : DESIGN + 1]

    image_out[...] = image
    sums = [norm_old, total_of(direction * image), total_of(residual * image), total_of(image * image)]
    spot = lax.broadcasted_iota(jnp.int32, (1, LANES), 1)
    line = jnp.zeros((1, LANES), F32)
    for k, value in enumerate(sums):
        line = jnp.where(spot == k, value, line)

    stages = [
        [at_z(d) for d in range(1, nz)],
        [at_cx(c, d) for c in range(nc) for d in range(nx) if c or d],
        [at_y(d) for d in range(1, ny)],
    ]
    exchanges = [
        [copy(vec.at[s], vec_in.at[s, i], v_send.at[s, i], v_recv.at[s, i], peer) for i, peer in enumerate(targets)]
        for s, targets in enumerate(stages)
    ]
    for s, copies in enumerate(exchanges):
        vec[s] = line
        for c in copies:
            c.start()
        for i, c in enumerate(copies):
            c.wait_recv()
            line = line + vec_in[s, i]

    sums_out[...] = line

    for r in range(1, nz):
        z_gather(r).wait_send()
    for r in range(nz):
        for i in range(1, nx):
            x_gather(r, i).wait_send()
    for r in range(1, ny):
        y_gather(r).wait_send()
        y_reduce(r).wait_send()
    for h in range(2):
        c_gather(h).wait_send()
        c_reduce(h).wait_send()
    for copies in exchanges:
        for c in copies:
            c.wait_send()


def finish(
    image_ref, sums_ref, solution_hbm, residual_hbm, direction_hbm,
    solution_out, residual_out, direction_out, given, made, load, store,
):
    inputs, outputs = (solution_hbm, residual_hbm, direction_hbm), (solution_out, residual_out, direction_out)
    loads = [pltpu.make_async_copy(src, given.at[i], load.at[i]) for i, src in enumerate(inputs)]
    stores = [pltpu.make_async_copy(made.at[i], dst, store.at[i]) for i, dst in enumerate(outputs)]
    for c in loads:
        c.start()
    norm_old, curvature, cross, square = (sums_ref[:, k : k + 1] for k in range(4))
    step_size = norm_old / curvature
    norm_new = norm_old - 2.0 * step_size * cross + step_size * step_size * square
    ratio = norm_new / norm_old
    for c in loads:
        c.wait()
    direction = given[2]
    made[0] = given[0] + step_size * direction
    stores[0].start()
    residual_next = given[1] - step_size * image_ref[...]
    made[1] = residual_next
    stores[1].start()
    made[2] = residual_next + ratio * direction
    stores[2].start()
    for c in stores:
        c.wait()


EVENTS = {0: (3,), 1: (4,), 3: (5,), 4: (6,), 6: (7,)}

PAIRS = 4


def build(dims, block, tile):
    ny, nc, nz, nx = dims
    width = nz * nx * block
    half = nc * ny * block // 2
    most = max(nz, ny, nc * nx)
    dma = pltpu.SemaphoreType.DMA
    vmem, hbm = pl.BlockSpec(memory_space=pltpu.VMEM), pl.BlockSpec(memory_space=pltpu.HBM)
    state = jax.ShapeDtypeStruct((block, DESIGN + 1), F32)
    inputs = [(block, DESIGN), (1, DESIGN)] + [(block, DESIGN + 1)] * 2

    def body(points, scales, solution, residual, direction):
        image, sums = pl.pallas_call(
            functools.partial(kernel, dims, block, tile),
            out_shape=(state, jax.ShapeDtypeStruct((1, LANES), F32)),
            in_specs=[hbm] * 4,
            out_specs=(vmem, vmem),
            scratch_shapes=[
                *[pltpu.VMEM(shape, F32) for shape in inputs],
                pltpu.VMEM((2, block, LANES), F32),
                pltpu.VMEM((2, nc, ny // 2 * block, LANES), F32),
                pltpu.VMEM((nz * nx, 2 * block, LANES), F32),
                pltpu.VMEM((2, half, 2 * LANES), BF16),
                *[pltpu.VMEM((width, LANES), BF16) for _ in range(6)],
                pltpu.VMEM((2, 4, half, tile), BF16),
                pltpu.VMEM((2, half, 2 * LANES), F32),
                pltpu.VMEM((2, nc, ny // 2 * block, LANES), F32),
                pltpu.VMEM((2, ny // 2 * block, LANES), F32),
                pltpu.VMEM((2, ny // 2 * block, LANES), F32),
                pltpu.VMEM((ny, block, LANES), F32),
                pltpu.VMEM((3, 1, LANES), F32),
                pltpu.VMEM((3, most, 1, LANES), F32),
                dma((4,)), dma((nz,)), dma((nz,)), dma((nz * nx,)), dma((nz * nx,)), dma((ny,)), dma((ny,)),
                dma((2,)), dma((2,)), dma((ny,)), dma((ny,)), dma((2,)), dma((2,)), dma((3, most)), dma((3, most)),
            ],
            compiler_params=pltpu.CompilerParams(
                collective_id=0, has_side_effects=True, vmem_limit_bytes=60 * 2**20
            ),
            name="iteration",
        )(points.T, scales.reshape(1, DESIGN), residual.T, direction.T)
        outs = pl.pallas_call(
            finish,
            out_shape=(state, state, state),
            in_specs=[vmem, vmem, hbm, hbm, hbm],
            out_specs=(hbm, hbm, hbm),
            scratch_shapes=[
                pltpu.VMEM((3, block, DESIGN + 1), F32), pltpu.VMEM((3, block, DESIGN + 1), F32), dma((3,)), dma((3,)),
            ],
            compiler_params=pltpu.CompilerParams(vmem_limit_bytes=60 * 2**20),
            name="update",
        )(image, sums, solution.T, residual.T, direction.T)
        return tuple(o.T for o in outs)

    return body


def solution(mesh, dims=None, block=80, tile=256):
    if dims is None:
        dims = (mesh.shape["row"] // 2, 2, mesh.shape["col"] // 4, 4)
    state = P(None, ("row", "col"))
    return jax.shard_map(
        build(dims, block, tile),
        mesh=mesh,
        in_specs=(state, P(), state, state, state),
        out_specs=(state, state, state),
        check_vma=False,
    )
```

```python
import functools
import math

import jax
import jax.numpy as jnp
from jax import lax
from jax.experimental import pallas as pl
from jax.experimental.pallas import tpu as pltpu
from jax.sharding import PartitionSpec as P

F32, BF16 = jnp.float32, jnp.bfloat16
MESH = pl.DeviceIdType.MESH
DESIGN = 96
LANES = 128
ROOT = math.sqrt(math.log2(math.e))
NT = (((1,), (1,)), ((), ()))
NN = (((1,), (0,)), ((), ()))
NORM, REST, ONE, ONE2 = 97, 98, 99, 100


def dot(a, b, dims):
    return lax.dot_general(a, b, dims, preferred_element_type=F32)


def split(x):
    high = x.astype(BF16)
    return high, (x - high.astype(F32)).astype(BF16)


def joined(x):
    high, low = split(x)
    return high.astype(F32) + low.astype(F32)


def rotate(index, shift, size):
    return lax.rem(index + shift, size)


def ring(size):
    return sorted(range(size), key=lambda d: (min(d, size - d), d))


def wide(a, b):
    return jnp.concatenate([a, b], axis=1)


def kernel(
    dims, block, tile,
    points_hbm, scales_hbm, residual_hbm, direction_hbm,
    image_out, sums_out,
    points_ref, scales_ref, residual_ref, direction_ref,
    pad, rows, cols, stream, coord_hi, coord_lo, slope_hi, slope_lo, grad_hi, grad_lo, pipe, acc,
    part, from_core, whole, from_y, vec, vec_in,
    load, z_send, z_recv, x_send, x_recv, y_send, y_recv, c_send, c_recv,
    yr_send, yr_recv, cr_send, cr_recv, v_send, v_recv,
):
    ny, nc, nz, nx = dims
    row, col = lax.axis_index("row"), lax.axis_index("col")
    y, core = row // nc, lax.rem(row, nc)
    z, x = col // nx, lax.rem(col, nx)
    ys, zs, xs = ring(ny), ring(nz), ring(nx)
    per = ny // 2
    half = nc * per * block
    items = 2 * nz * nx * block // tile

    def at_z(shift):
        return (row, rotate(z, shift, nz) * nx + x)

    def at_x(shift):
        return (row, z * nx + rotate(x, shift, nx))

    def at_y(shift):
        return (rotate(y, shift, ny) * nc + core, col)

    def at_cx(dc, dx):
        return (y * nc + rotate(core, dc, nc), z * nx + rotate(x, dx, nx))

    inputs = [
        (points_hbm, points_ref), (scales_hbm, scales_ref), (direction_hbm, direction_ref),
        (residual_hbm, residual_ref),
    ]
    loads = [pltpu.make_async_copy(src, dst, load.at[i]) for i, (src, dst) in enumerate(inputs)]
    for c in loads:
        c.start()

    peers = [at_z(d) for d in range(1, nz)] + [at_y(d) for d in range(1, ny)]
    peers += [at_cx(c, d) for c in range(nc) for d in range(nx) if c or d]
    barrier = pltpu.get_barrier_semaphore()
    for peer in peers:
        pl.semaphore_signal(barrier, inc=1, device_id=peer, device_id_type=MESH)

    lane = lax.broadcasted_iota(jnp.int32, (block, LANES), 1)
    for c in loads[:3]:
        c.wait()
    pad[...] = jnp.zeros_like(pad)
    pad[0, :, 1 : DESIGN + 1] = points_ref[...] * (jnp.sqrt(2.0 * scales_ref[...]) * ROOT)
    pad[1, :, 0 : DESIGN + 1] = direction_ref[...]
    coords = joined(pad[0])
    norm = -0.5 * jnp.sum(coords * coords, axis=1, keepdims=True)
    norm_main = joined(norm)
    norm_rest = norm - norm_main
    own_row = jnp.where(lane == NORM, norm_main, coords)
    own_row = jnp.where(lane == REST, norm_rest, own_row)
    own_row = jnp.where((lane == ONE) | (lane == ONE2), 1.0, own_row)
    own_col = jnp.where(lane == ONE, norm_main, coords)
    own_col = jnp.where(lane == ONE2, norm_rest, own_col)
    own_col = jnp.where((lane == NORM) | (lane == REST) | (lane == 0), 1.0, own_col)
    field = pad[1]
    grads = joined(jnp.where(lane >= 1, field * (1.0 / ROOT), 0.0))
    value = field[:, 0:1] - jnp.sum(coords * grads, axis=1, keepdims=True)
    value_main = joined(value)
    own_slope = jnp.where(lane == ONE, value_main, grads)
    own_slope = jnp.where(lane == ONE2, value - value_main, own_slope)
    rows[0, 0, 0:block] = own_row
    cols[0, 0:block] = own_col
    cols[0, block:] = own_slope

    pl.semaphore_wait(barrier, len(peers))

    def copy(src, dst, send, recv, peer):
        return pltpu.make_async_remote_copy(
            src_ref=src, dst_ref=dst, send_sem=send, recv_sem=recv, device_id=peer, device_id_type=MESH
        )

    def y_gather(r):
        h, k = divmod(r, per)
        there = rows.at[h, 0, pl.ds(k * block, block)]
        return copy(rows.at[0, 0, pl.ds(0, block)], there, y_send.at[r], y_recv.at[r], at_y(ny - ys[r]))

    def c_gather(h):
        return copy(rows.at[h, 0], rows.at[h, 1], c_send.at[h], c_recv.at[h], at_cx(1, 0))

    def z_gather(r):
        return copy(cols.at[0], cols.at[r * nx], z_send.at[r], z_recv.at[r], at_z(nz - zs[r]))

    def x_gather(r, i):
        here, there = cols.at[r * nx], cols.at[r * nx + i]
        return copy(here, there, x_send.at[r * nx + i], x_recv.at[r * nx + i], at_x(nx - xs[i]))

    def pass_on(r):
        if r:
            z_gather(r).wait_recv()
        for i in range(1, nx):
            x_gather(r, i).start()

    for r in range(1, per):
        y_gather(r).start()
    for r in range(1, min(nz, 3)):
        z_gather(r).start()
    pass_on(0)
    for r in range(3, nz):
        z_gather(r).start()
    for r in range(per, ny):
        y_gather(r).start()
    acc[...] = jnp.zeros_like(acc)
    for c in loads[3:]:
        c.wait()
    residual, direction = residual_ref[...], direction_ref[...]

    def total_of(a):
        return jnp.sum(jnp.sum(a, axis=1, keepdims=True), axis=0, keepdims=True)

    norm_old = total_of(residual * residual)

    def factor(s, _):
        @pl.when(lax.rem(s, nx) > 0)
        def _():
            copy(cols.at[0], cols.at[s], x_send.at[s], x_recv.at[s], at_x(1)).wait_recv()

        here = pl.ds(pl.multiple_of(s * block, block), block)
        slope = cols[s, block:]
        coord_hi[here], coord_lo[here] = split(cols[s, 0:block])
        slope_hi[here], slope_lo[here] = split(slope)
        grad_hi[here], grad_lo[here] = split(slope * (ROOT * ROOT))
        return 0

    def rows_in(h):
        for r in range(h * per, (h + 1) * per):
            if r:
                y_gather(r).wait_recv()
        c_gather(h).start()
        c_gather(h).wait_recv()
        for c in range(nc):
            here = pl.ds(c * per * block, per * block)
            stream[h, here, 0:LANES], stream[h, here, LANES:] = split(rows[h, c])

    def place(n):
        def since(c):
            return (n + items - c) // items

        pair = since(2) - since(2 + 2 * PAIRS)
        last = since(2 + PAIRS + items // 2)
        far = since(2 + 2 * PAIRS) - last
        h = pair * lax.rem(n, 2) + far
        t = (1 - since(2)) * n + pair * (n // 2 + 1 - 2 * lax.rem(n, 2))
        t = t + far * (n - 2 - PAIRS) + last * (n - items // 2)
        fresh = (1 - h) * (1 - last) + since(4 + 2 * PAIRS) - last
        return h, t, fresh

    def columns(t):
        return pl.ds(pl.multiple_of(t * tile, tile), tile)

    def first(n):
        h, t, fresh = place(n)
        low = (t * tile + block - 1) // block
        high = ((t + 1) * tile + block - 1) // block
        lax.fori_loop(low, low + fresh * (high - low), factor, 0)
        c, left = columns(t), stream[h]
        chi, clo, shi, slo = coord_hi[c], coord_lo[c], slope_hi[c], slope_lo[c]
        weight = jnp.exp2(dot(left, wide(chi, chi), NT) + dot(left, wide(clo, clo), NT))
        weighted = weight * (dot(left, wide(shi, shi), NT) + dot(left, wide(slo, slo), NT))
        return (*split(weighted), *split(weight))

    def second(n):
        h, t, _ = place(n)
        c, slot = columns(t), lax.rem(n, 2)
        by_coord, by_grad = wide(coord_hi[c], coord_lo[c]), wide(grad_hi[c], grad_lo[c])
        term = dot(pipe[slot, 0], by_coord, NN) + dot(pipe[slot, 1], by_coord, NN)
        term = term + dot(pipe[slot, 2], by_grad, NN) + dot(pipe[slot, 3], by_grad, NN)
        acc[h] = acc[h] + term

    def keep(n, values):
        slot = lax.rem(n, 2)
        for i, value in enumerate(values):
            pipe[slot, i] = value

    def c_reduce(h):
        return copy(part.at[h, 1], from_core.at[h], cr_send.at[h], cr_recv.at[h], at_cx(1, 0))

    def y_reduce(r):
        h, k = divmod(r, per)
        return copy(whole.at[h, pl.ds(k * block, block)], from_y.at[r], yr_send.at[r], yr_recv.at[r], at_y(ys[r]))

    def to_core(h):
        for c in range(nc):
            here = pl.ds(c * per * block, per * block)
            part[h, c] = acc[h, here, 0:LANES] + acc[h, here, LANES:]
        c_reduce(h).start()

    def to_y(h):
        c_reduce(h).wait_recv()
        whole[h] = part[h, 0] + from_core[h]
        for r in reversed(range(h * per, (h + 1) * per)):
            if r:
                y_reduce(r).start()

    def body(n, _):
        for at, ranks in events.items():

            @pl.when(n == at)
            def _(ranks=ranks):
                for r in ranks:
                    pass_on(r)

        @pl.when(n == 2)
        def _():
            rows_in(1)

        @pl.when(n == 2 + PAIRS + items // 2)
        def _():
            to_core(1)

        @pl.when(n == 3 + PAIRS + items // 2)
        def _():
            to_y(1)

        values = first(n + 1)
        second(n)
        keep(n + 1, values)
        return 0

    early = [r for r in (1, 2) if r < nz]
    events = {at: [r for r in ranks if r < nz] for at, ranks in EVENTS.items()}
    for r in early:
        pass_on(r)
    rows_in(0)
    keep(0, first(0))
    lax.fori_loop(0, items - 1, body, 0)
    second(items - 1)
    to_core(0)
    to_y(0)

    total = whole[0, 0:block]
    for r in range(1, ny):
        y_reduce(r).wait_recv()
        total = total + from_y[r]
    image = jnp.where(lane == 0, total, (total - own_row * total[:, 0:1]) * (1.0 / ROOT))[:, 0 : DESIGN + 1]

    image_out[...] = image
    sums = [norm_old, total_of(direction * image), total_of(residual * image), total_of(image * image)]
    spot = lax.broadcasted_iota(jnp.int32, (1, LANES), 1)
    line = jnp.zeros((1, LANES), F32)
    for k, value in enumerate(sums):
        line = jnp.where(spot == k, value, line)

    stages = [
        [at_cx(c, d) for c in range(nc) for d in range(nx) if c or d],
        [at_z(d) for d in range(1, nz)],
        [at_y(d) for d in range(1, ny)],
    ]
    exchanges = [
        [copy(vec.at[s], vec_in.at[s, i], v_send.at[s, i], v_recv.at[s, i], peer) for i, peer in enumerate(targets)]
        for s, targets in enumerate(stages)
    ]
    for s, copies in enumerate(exchanges):
        vec[s] = line
        for c in copies:
            c.start()
        for i, c in enumerate(copies):
            c.wait_recv()
            line = line + vec_in[s, i]

    sums_out[...] = line

    for r in range(1, nz):
        z_gather(r).wait_send()
    for r in range(nz):
        for i in range(1, nx):
            x_gather(r, i).wait_send()
    for r in range(1, ny):
        y_gather(r).wait_send()
        y_reduce(r).wait_send()
    for h in range(2):
        c_gather(h).wait_send()
        c_reduce(h).wait_send()
    for copies in exchanges:
        for c in copies:
            c.wait_send()


def finish(
    image_ref, sums_ref, solution_hbm, residual_hbm, direction_hbm,
    solution_out, residual_out, direction_out, given, made, load, store,
):
    inputs, outputs = (solution_hbm, residual_hbm, direction_hbm), (solution_out, residual_out, direction_out)
    loads = [pltpu.make_async_copy(src, given.at[i], load.at[i]) for i, src in enumerate(inputs)]
    stores = [pltpu.make_async_copy(made.at[i], dst, store.at[i]) for i, dst in enumerate(outputs)]
    for c in loads:
        c.start()
    norm_old, curvature, cross, square = (sums_ref[:, k : k + 1] for k in range(4))
    step_size = norm_old / curvature
    norm_new = norm_old - 2.0 * step_size * cross + step_size * step_size * square
    ratio = norm_new / norm_old
    for c in loads:
        c.wait()
    direction = given[2]
    made[0] = given[0] + step_size * direction
    stores[0].start()
    residual_next = given[1] - step_size * image_ref[...]
    made[1] = residual_next
    stores[1].start()
    made[2] = residual_next + ratio * direction
    stores[2].start()
    for c in stores:
        c.wait()


EVENTS = {0: (3,), 1: (4,), 3: (5,), 4: (6,), 6: (7,)}

PAIRS = 4


def build(dims, block, tile):
    ny, nc, nz, nx = dims
    width = nz * nx * block
    half = nc * ny * block // 2
    most = max(nz, ny, nc * nx)
    dma = pltpu.SemaphoreType.DMA
    vmem, hbm = pl.BlockSpec(memory_space=pltpu.VMEM), pl.BlockSpec(memory_space=pltpu.HBM)
    state = jax.ShapeDtypeStruct((block, DESIGN + 1), F32)
    inputs = [(block, DESIGN), (1, DESIGN)] + [(block, DESIGN + 1)] * 2

    def body(points, scales, solution, residual, direction):
        image, sums = pl.pallas_call(
            functools.partial(kernel, dims, block, tile),
            out_shape=(state, jax.ShapeDtypeStruct((1, LANES), F32)),
            in_specs=[hbm] * 4,
            out_specs=(vmem, vmem),
            scratch_shapes=[
                *[pltpu.VMEM(shape, F32) for shape in inputs],
                pltpu.VMEM((2, block, LANES), F32),
                pltpu.VMEM((2, nc, ny // 2 * block, LANES), F32),
                pltpu.VMEM((nz * nx, 2 * block, LANES), F32),
                pltpu.VMEM((2, half, 2 * LANES), BF16),
                *[pltpu.VMEM((width, LANES), BF16) for _ in range(6)],
                pltpu.VMEM((2, 4, half, tile), BF16),
                pltpu.VMEM((2, half, 2 * LANES), F32),
                pltpu.VMEM((2, nc, ny // 2 * block, LANES), F32),
                pltpu.VMEM((2, ny // 2 * block, LANES), F32),
                pltpu.VMEM((2, ny // 2 * block, LANES), F32),
                pltpu.VMEM((ny, block, LANES), F32),
                pltpu.VMEM((3, 1, LANES), F32),
                pltpu.VMEM((3, most, 1, LANES), F32),
                dma((4,)), dma((nz,)), dma((nz,)), dma((nz * nx,)), dma((nz * nx,)), dma((ny,)), dma((ny,)),
                dma((2,)), dma((2,)), dma((ny,)), dma((ny,)), dma((2,)), dma((2,)), dma((3, most)), dma((3, most)),
            ],
            compiler_params=pltpu.CompilerParams(
                collective_id=0, has_side_effects=True, vmem_limit_bytes=60 * 2**20
            ),
            name="iteration",
        )(points.T, scales.reshape(1, DESIGN), residual.T, direction.T)
        outs = pl.pallas_call(
            finish,
            out_shape=(state, state, state),
            in_specs=[vmem, vmem, hbm, hbm, hbm],
            out_specs=(hbm, hbm, hbm),
            scratch_shapes=[
                pltpu.VMEM((3, block, DESIGN + 1), F32), pltpu.VMEM((3, block, DESIGN + 1), F32), dma((3,)), dma((3,)),
            ],
            compiler_params=pltpu.CompilerParams(vmem_limit_bytes=60 * 2**20),
            name="update",
        )(image, sums, solution.T, residual.T, direction.T)
        return tuple(o.T for o in outs)

    return body


def solution(mesh, dims=None, block=80, tile=256):
    if dims is None:
        dims = (mesh.shape["row"] // 2, 2, mesh.shape["col"] // 4, 4)
    state = P(None, ("row", "col"))
    return jax.shard_map(
        build(dims, block, tile),
        mesh=mesh,
        in_specs=(state, P(), state, state, state),
        out_specs=(state, state, state),
        check_vma=False,
    )
```
